32 devices in a mesh: dp: 8 (over z, x), ctx: 4 (over y, core).
Axes of the slice: x: 2, y: 2, z: 4, core: 2. Of those that a mesh axis runs over, the one named last changes fastest.
Arguments:
- hidden_in: float32 [16, 1024, 768], P('dp', 'ctx'), may hold values from -6 to 6
- doc_positions: int32 [16, 1024], P('dp', 'ctx'), may hold values from 0 to 895, as said below
- attn_gain: bfloat16 [768], P(('dp', 'ctx')), may hold values from 0.099609375 to 1.8984375
- qkv_weight: bfloat16 [768, 2304], P(('dp', 'ctx')), may hold values from -0.21875 to 0.21875
- out_weight: bfloat16 [768, 768], P(('dp', 'ctx')), may hold values from -2 to 2
- mlp_gain: bfloat16 [768], P(('dp', 'ctx')), may hold values from 0.099609375 to 1.8984375
- inner_weight: bfloat16 [768, 2304], P(('dp', 'ctx')), may hold values from -0.21875 to 0.21875
- outer_weight: bfloat16 [1152, 768], P(None, ('dp', 'ctx')), may hold values from -0.25 to 0.25
- grad_out: float32 [16, 1024, 768], P('dp', 'ctx'), may hold values from -6 to 6
Outputs:
- output: float32 [16, 1024, 768], P('dp', 'ctx')
- input_grad: float32 [16, 1024, 768], P('dp', 'ctx')
- attn_gain_grad: float32 [768], P(('dp', 'ctx'))
- qkv_weight_grad: float32 [768, 2304], P(('dp', 'ctx'))
- out_weight_grad: float32 [768, 768], P(('dp', 'ctx'))
- mlp_gain_grad: float32 [768], P(('dp', 'ctx'))
- inner_weight_grad: float32 [768, 2304], P(('dp', 'ctx'))
- outer_weight_grad: float32 [1152, 768], P(None, ('dp', 'ctx'))
The draws below stay inside these ranges and needn't reach their ends.
Inputs may be any that keep to these rules, and one draw needn't show every extreme that they name: `doc_positions`: each row counts 0, 1, 2, ... through each document of its sequence; inner documents hold 102 to 896 tokens, the first and last of a sequence may be shorter; in each group of 2 sequences along dp one document of one sequence starts on the first device of ctx and ends on the last, and has 896 tokens.
All inputs are finite; a program needn't handle non-finite values.
Results may differ from the reference program's by a relative error of at most 0.015.
Values may be sent and summed in bfloat16 or wider, within the bound.
No kernel may reach another device: no remote copies, remote signals or barrier semaphores. Data moves between devices by JAX's collectives and lax.ppermute only.
A program may use at most 256 MiB of HBM per device.

```python
import math
import jax
import jax.numpy as jnp
from jax import lax

D = 768
HEADS = 12
HEAD_DIM = 64
FF = 1152
SEQ_DEV = 256
SEQS_DP = 2
SEQ_LEN = 1024
SEQS = 16
DOC_LEAST = 102
DOC_MOST = 896


def draw_doc_positions(key, part):
    key = jax.random.fold_in(key, 11)
    key_len, key_pick, key_offset = jax.random.split(key, 3)
    piece_count = SEQ_LEN // DOC_LEAST + 2
    lengths = jax.random.randint(key_len, (SEQS, piece_count), DOC_LEAST, DOC_MOST + 1)
    bounds = jnp.concatenate([jnp.zeros((SEQS, 1), jnp.int32), jnp.cumsum(lengths, axis=1).astype(jnp.int32)], axis=1)
    token_index = jnp.arange(SEQ_LEN, dtype=jnp.int32)
    below = bounds[:, None, :] <= token_index[None, :, None]
    start_free = jnp.max(jnp.where(below, bounds[:, None, :], 0), axis=2)
    chosen = jax.random.randint(key_pick, (SEQS // SEQS_DP,), 0, SEQS_DP)
    offset = jax.random.randint(key_offset, (SEQS,), 0, SEQ_DEV // 2 + 1)
    finish = offset + DOC_MOST
    start_long = jnp.where(token_index[None, :] < offset[:, None], 0, jnp.where(token_index[None, :] < finish[:, None], offset[:, None], finish[:, None]))
    slot_in_group = jnp.arange(SEQS, dtype=jnp.int32) % SEQS_DP
    spanning = (slot_in_group == jnp.repeat(chosen, SEQS_DP))[:, None]
    starts = jnp.where(spanning, start_long, start_free)
    return (token_index[None, :] - starts).astype(jnp.int32)


def steps_of(rng, dims, cuts, least, largest):
    gain, own = 1.0, jax.random.fold_in(rng, 6)
    for dim, shards_of in cuts:
        steps = jnp.exp(jax.random.uniform(jax.random.fold_in(own, dim), (shards_of,), jnp.float32, least / len(cuts), largest / len(cuts)))
        gain = gain * jnp.repeat(steps, dims[dim] // shards_of).reshape([-1 if axis == dim else 1 for axis in range(len(dims))])
    return gain


def centred(stream_key, dims, width, bound, cuts=(), kind=jnp.bfloat16):
    loudness = steps_of(stream_key, dims, cuts, -0.22, 0.18) if cuts else 1.0
    array = jax.random.normal(stream_key, dims, jnp.float32) * width * loudness
    return jnp.minimum(jnp.maximum(array, -bound), bound).astype(kind)


def setup_inputs(seed: int = 0) -> dict:
    seeds = jax.random.split(jax.random.key(seed), 10)
    hidden_in = centred(seeds[0], (SEQS, SEQ_LEN, D), 1.0, 6.0, ((0, 8), (1, 4)), jnp.float32)
    doc_positions = draw_doc_positions(jax.random.fold_in(seeds[9], 71), 0)
    attn_gain = jnp.clip(1.0 + 0.18 * jax.random.normal(seeds[2], (D,), jnp.float32), 0.099609375, 1.8984375).astype(jnp.bfloat16)
    qkv_weight = centred(seeds[3], (D, 3 * D), D ** -0.5, 0.21875, ((0, 32),))
    out_weight = centred(seeds[4], (D, D), 8 ** -0.5, 2.0, ((0, 32),))
    mlp_gain = jnp.clip(1.0 + 0.18 * jax.random.normal(seeds[5], (D,), jnp.float32), 0.099609375, 1.8984375).astype(jnp.bfloat16)
    inner_weight = centred(seeds[6], (D, 2 * FF), D ** -0.5, 0.21875, ((0, 32),))
    outer_weight = centred(seeds[7], (FF, D), (FF // 2) ** -0.5, 0.25, ((1, 32),))
    grad_out = centred(seeds[8], (SEQS, SEQ_LEN, D), 1.0, 6.0, ((0, 8), (1, 4)), jnp.float32)
    return dict(hidden_in=hidden_in, doc_positions=doc_positions, attn_gain=attn_gain, qkv_weight=qkv_weight, out_weight=out_weight, mlp_gain=mlp_gain, inner_weight=inner_weight, outer_weight=outer_weight, grad_out=grad_out)


EPS = 1e-05
THETA = 160000.0
NEG_FILL = -1e+30
HIGH = lax.Precision.HIGHEST

@jax.custom_vjp
def low(v):
    return lax.optimization_barrier(v.astype(jnp.bfloat16)).astype(jnp.float32)

@jax.custom_vjp
def low_back(v):
    return v

def low_keep(v):
    return (low(v), None)

def low_pass(kept, grad):
    return (grad,)

def back_keep(v):
    return (v, None)

def back_low(kept, grad):
    return (low(grad),)
low.defvjp(low_keep, low_pass)
low_back.defvjp(back_keep, back_low)

def normalize(rows_in):
    row_mean = lax.optimization_barrier(jnp.mean(rows_in, axis=-1, keepdims=True))
    centered = rows_in - row_mean
    variance = lax.optimization_barrier(jnp.mean(centered * centered, axis=-1, keepdims=True))
    inv_std = lax.rsqrt(variance + EPS)
    return centered * inv_std

def rope_tables(positions):
    half_dim = HEAD_DIM // 2
    exponent = jnp.arange(half_dim, dtype=jnp.float32) * (2.0 / HEAD_DIM)
    frequency = jnp.power(jnp.float32(THETA), -exponent)
    angles = positions.astype(jnp.float32)[..., None] * frequency
    return (jnp.cos(angles)[..., None, :], jnp.sin(angles)[..., None, :])

def rotate(values, cos_table, sine_table):
    half_dim = values.shape[-1] // 2
    front_half = values[..., :half_dim]
    back_half = values[..., half_dim:]
    return jnp.concatenate([front_half * cos_table - back_half * sine_table, back_half * cos_table + front_half * sine_table], axis=-1)

def layer(rows_in, params, positions):
    attn_gain, qkv_weight, out_weight, mlp_gain, inner_weight, outer_weight = params
    length = rows_in.shape[0]
    scale_factor = 1.0 / math.sqrt(HEAD_DIM)
    doc_start = jnp.arange(length, dtype=jnp.int32) - positions.astype(jnp.int32)
    same_doc = doc_start[:, None] == doc_start[None, :]
    first_in = low(normalize(rows_in) * attn_gain)
    qkv_rows = low_back(jnp.dot(first_in, qkv_weight, precision=HIGH))
    parted = qkv_rows.reshape(length, 3, HEADS, HEAD_DIM)
    cos_table, sine_table = rope_tables(positions)
    queries = low(rotate(parted[:, 0], cos_table, sine_table))
    keys_r = low(rotate(parted[:, 1], cos_table, sine_table))
    values_r = low(parted[:, 2])
    scores = low_back(jnp.einsum('qhd,khd->hqk', queries, keys_r, precision=HIGH) * scale_factor)
    masked = jnp.where(same_doc[None], scores, NEG_FILL)
    soft_probs = low(jax.nn.softmax(masked, axis=-1))
    context = jnp.einsum('hqk,khd->qhd', soft_probs, values_r, precision=HIGH).reshape(length, HEADS * HEAD_DIM)
    context = low(low_back(context))
    middle = rows_in + low_back(jnp.dot(context, out_weight, precision=HIGH))
    second_in = low(normalize(middle) * mlp_gain)
    gate_up = low_back(jnp.dot(second_in, inner_weight, precision=HIGH))
    gated = low(jax.nn.gelu(gate_up[:, :FF], approximate=False) * gate_up[:, FF:])
    return middle + low_back(jnp.dot(gated, outer_weight, precision=HIGH))

def reference(hidden_in, doc_positions, attn_gain, qkv_weight, out_weight, mlp_gain, inner_weight, outer_weight, grad_out):
    params = tuple((w.astype(jnp.float32) for w in (attn_gain, qkv_weight, out_weight, mlp_gain, inner_weight, outer_weight)))
    zeros = jax.tree.map(jnp.zeros_like, params)

    def one_sequence(totals, pieces):
        seq_rows, seq_pos, seq_grad = pieces
        result, pull = jax.vjp(lambda rows_in, weights: layer(rows_in, weights, seq_pos), seq_rows, params)
        rows_grad, weight_grads = pull(seq_grad)
        totals = jax.tree.map(jnp.add, totals, weight_grads)
        return (totals, (result, rows_grad))
    grads, (output, input_grad) = lax.scan(one_sequence, zeros, (hidden_in, doc_positions, grad_out))
    return (output, input_grad, grads[0], grads[1], grads[2], grads[3], grads[4], grads[5])
```

```python
import functools
import math

import jax
import jax.numpy as jnp
from jax import lax
from jax.experimental import pallas as pl
from jax.experimental.pallas import tpu as pltpu
from jax.sharding import PartitionSpec as P

HEADS = 12
HEAD_DIM = 64
FF = 1152
LANES = 128

EPS = 1e-05
THETA = 160000.0
FAR = -(2.0**99)
BITS = 16

AXES = ("dp", "ctx")
BF = jnp.bfloat16
F32 = jnp.float32

NT = (((1,), (1,)), ((), ()))
TN = (((0,), (0,)), ((), ()))
NN = (((1,), (0,)), ((), ()))


def mm(lhs, rhs, dims=NN):
    return lax.dot_general(lhs, rhs, dims, preferred_element_type=F32)


def turn(rows, cos_table, sine_table, front):
    ahead = pltpu.roll(rows, LANES - HEAD_DIM // 2, 1)
    behind = pltpu.roll(rows, HEAD_DIM // 2, 1)
    return rows * cos_table, jnp.where(front, ahead, behind) * sine_table


def lane_masks(rows):
    lane = lax.broadcasted_iota(jnp.int32, (rows, LANES), 1)
    return lane < HEAD_DIM, (lane % HEAD_DIM) < HEAD_DIM // 2


def attend_kernel(block, qkv_ref, cos_ref, sin_ref, qtag_ref, ktag_ref, kept_ref, ctx_ref, lse_ref):
    length = qkv_ref.shape[0]
    low, front = lane_masks(length)
    cos_table, sine_table = cos_ref[...], sin_ref[...]
    plain, crossed = turn(qkv_ref[:, :LANES], cos_table, sine_table, front)
    kept_ref[:, :LANES] = ((plain + crossed) * (1.0 / math.sqrt(HEAD_DIM))).astype(BF)
    plain, crossed = turn(qkv_ref[:, LANES : 2 * LANES], cos_table, sine_table, front)
    keys = (plain + crossed).astype(BF)
    kept_ref[:, LANES : 2 * LANES] = keys
    values = qkv_ref[:, 2 * LANES :].astype(BF)
    kept_ref[:, 2 * LANES :] = values
    values = values.astype(F32)
    ktag = ktag_ref[...]
    low_rows = lax.broadcasted_iota(jnp.int32, (LANES, block), 0) < HEAD_DIM
    low_block = low[:block]
    keys_of = (jnp.where(low, keys, ktag), jnp.where(low, ktag, keys))
    values_of = (
        jnp.transpose(jnp.where(low, values, 1.0)).astype(BF),
        jnp.transpose(jnp.where(low, 1.0, values)).astype(BF),
    )
    for start in range(0, length, block):
        queries = kept_ref[start : start + block, :LANES]
        qtag = qtag_ref[start : start + block, :]
        queries_of = (jnp.where(low_block, queries, qtag), jnp.where(low_block, qtag, queries))
        parts = []
        for head in range(2):
            scores = mm(keys_of[head], queries_of[head], NT)
            top = jnp.max(scores, axis=0, keepdims=True)
            terms = jnp.exp(scores - top).astype(BF)
            mixed = mm(values_of[head], terms)
            total = mixed[HEAD_DIM : HEAD_DIM + 1] if head == 0 else mixed[:1]
            lse_ref[0, head : head + 1, start : start + block] = top + jnp.log(total)
            parts.append(mixed / total)
        joined = jnp.where(low_rows, parts[0], parts[1])
        ctx_ref[start : start + block, :] = jnp.transpose(joined).astype(BF)


def attend_back_kernel(
    block, kept_ref, ctx_ref, grad_ref, lse_ref, cos_ref, sin_ref, qtag_ref, ktag_ref, out_ref, acc_ref
):
    length = kept_ref.shape[0]
    low, front = lane_masks(length)
    zero = jnp.zeros((length, LANES), BF)
    queries = kept_ref[:, :LANES]
    grads = grad_ref[...]
    qtag = qtag_ref[...]
    queries_of = (jnp.where(low, queries, qtag), jnp.where(low, qtag, queries))
    clean_of = (jnp.where(low, queries, zero), jnp.where(low, zero, queries))
    grads_of = (jnp.where(low, grads, zero), jnp.where(low, zero, grads))
    product = jnp.transpose(grads.astype(F32) * ctx_ref[...].astype(F32))
    delta_of = (
        jnp.sum(product[:HEAD_DIM], axis=0, keepdims=True),
        jnp.sum(product[HEAD_DIM:], axis=0, keepdims=True),
    )
    low_block = low[:block]
    zero_block = zero[:block]
    for start in range(0, length, block):
        rows = slice(start, start + block)
        keys = kept_ref[rows, LANES : 2 * LANES]
        values = kept_ref[rows, 2 * LANES :]
        ktag = ktag_ref[rows, :]
        keys_of = (jnp.where(low_block, keys, ktag), jnp.where(low_block, ktag, keys))
        keys_f = keys.astype(F32)
        key_grad = value_grad = query_part = None
        for head in range(2):
            scores = mm(keys_of[head], queries_of[head], NT)
            probs = jnp.exp(scores - lse_ref[0, head : head + 1, :])
            prob_grad = mm(values, grads_of[head], NT)
            score_grad = (probs * (prob_grad - delta_of[head])).astype(BF)
            value_term = mm(probs.astype(BF), grads_of[head])
            key_term = mm(score_grad, clean_of[head])
            mine = low_block if head == 0 else jnp.logical_not(low_block)
            turned = jnp.transpose(jnp.where(mine, keys_f, 0.0)).astype(BF)
            query_term = mm(turned, score_grad)
            value_grad = value_term if head == 0 else value_grad + value_term
            key_grad = key_term if head == 0 else key_grad + key_term
            query_part = query_term if head == 0 else query_part + query_term
        acc_ref[...] = query_part if start == 0 else acc_ref[...] + query_part
        plain, crossed = turn(key_grad, cos_ref[rows, :], sin_ref[rows, :], front[:block])
        out_ref[rows, LANES : 2 * LANES] = (plain - crossed).astype(BF)
        out_ref[rows, 2 * LANES :] = value_grad.astype(BF)
    query_grad = jnp.transpose(acc_ref[...]) * (1.0 / math.sqrt(HEAD_DIM))
    plain, crossed = turn(query_grad, cos_ref[...], sin_ref[...], front)
    out_ref[:, :LANES] = (plain - crossed).astype(BF)


def whole_block(length):
    return pl.BlockSpec((length, LANES), lambda j: (0, 0))


def column_block(length, width):
    return pl.BlockSpec((length, width), lambda j: (0, j))


def attend(qkv_rows, cos_table, sine_table, qtag, ktag):
    length = qkv_rows.shape[0]
    pairs = qkv_rows.shape[1] // (3 * LANES)
    block = 256
    return pl.pallas_call(
        functools.partial(attend_kernel, block),
        grid=(pairs,),
        in_specs=[column_block(length, 3 * LANES)] + [whole_block(length)] * 4,
        out_specs=[
            column_block(length, 3 * LANES),
            column_block(length, LANES),
            pl.BlockSpec((1, 2, length), lambda j: (j, 0, 0)),
        ],
        out_shape=[
            jax.ShapeDtypeStruct((length, pairs * 3 * LANES), BF),
            jax.ShapeDtypeStruct((length, pairs * LANES), BF),
            jax.ShapeDtypeStruct((pairs, 2, length), F32),
        ],
        compiler_params=pltpu.CompilerParams(vmem_limit_bytes=48 * 1024 * 1024),
        cost_estimate=pl.CostEstimate(
            flops=pairs * 2 * 2 * 2 * length * length * 256,
            bytes_accessed=length * pairs * LANES * 20,
            transcendentals=pairs * 2 * length * length,
        ),
    )(qkv_rows, cos_table, sine_table, qtag, ktag)


def attend_back(kept, context, context_grad, lse, cos_table, sine_table, qtag, ktag):
    length = kept.shape[0]
    pairs = kept.shape[1] // (3 * LANES)
    block = 256
    return pl.pallas_call(
        functools.partial(attend_back_kernel, block),
        grid=(pairs,),
        in_specs=[
            column_block(length, 3 * LANES),
            column_block(length, LANES),
            column_block(length, LANES),
            pl.BlockSpec((1, 2, length), lambda j: (j, 0, 0)),
        ]
        + [whole_block(length)] * 4,
        out_specs=column_block(length, 3 * LANES),
        out_shape=jax.ShapeDtypeStruct((length, pairs * 3 * LANES), BF),
        scratch_shapes=[pltpu.VMEM((LANES, length), F32)],
        compiler_params=pltpu.CompilerParams(vmem_limit_bytes=48 * 1024 * 1024),
        cost_estimate=pl.CostEstimate(
            flops=pairs * 2 * 5 * 2 * length * length * 256,
            bytes_accessed=length * pairs * LANES * 20,
            transcendentals=pairs * 2 * length * length,
        ),
    )(kept, context, context_grad, lse, cos_table, sine_table, qtag, ktag)


class Plan:
    def __init__(self, dp, ctx, seqs):
        self.dp, self.ctx = dp, ctx
        self.group = ctx // seqs
        self.fast = (dp, ctx, self.group) == (8, 4, 2)
        self.ctx_id = lax.axis_index("ctx")
        self.dp_id = lax.axis_index("dp")
        self.member = self.ctx_id % self.group
        self.seq = self.ctx_id // self.group

    def permute(self, array, target):
        pairs = []
        for dp in range(self.dp):
            for ctx in range(self.ctx):
                far_dp, far_ctx = target(dp, ctx)
                pairs.append((dp * self.ctx + ctx, far_dp * self.ctx + far_ctx))
        return lax.ppermute(array, AXES, pairs)

    def swap(self, array):
        return self.permute(array, lambda dp, ctx: (dp, (ctx + self.group) % self.ctx))

    def shift(self, array, step):
        size = self.group
        return self.permute(
            array, lambda dp, ctx: (dp, ctx // size * size + (ctx % size + step) % size)
        )

    def over_z(self, array, step):
        return self.permute(array, lambda dp, ctx: ((dp + 2 * step) % 8, ctx))

    def over_x(self, array):
        return self.permute(array, lambda dp, ctx: (dp ^ 1, ctx))

    def over_y(self, array):
        return self.permute(array, lambda dp, ctx: (dp, ctx ^ 2))

    def over_core(self, array):
        return self.permute(array, lambda dp, ctx: (dp, ctx ^ 1))

    @property
    def bits(self):
        return self.dp_id // 2, self.dp_id % 2, self.ctx_id // 2, self.ctx_id % 2


def in_order(mine, other, bit, axis):
    return jnp.where(
        bit == 0, jnp.stack([mine, other], axis=axis), jnp.stack([other, mine], axis=axis)
    )


def pick(array, index, axis):
    return lax.dynamic_index_in_dim(array, index, axis, keepdims=False)


def gather_z(plan, shard):
    z = plan.bits[0]
    parts = [shard] + [plan.over_z(shard, step) for step in (1, 2, 3)]
    ring = jnp.stack([parts[3], parts[2], parts[1], parts[0], parts[3], parts[2], parts[1]])
    return lax.dynamic_slice_in_dim(ring, 3 - z, 4, 0)


def gather_xy(plan, held):
    _, x, y, _ = plan.bits
    held = in_order(held, plan.over_x(held), x, 1)
    return in_order(held, plan.over_y(held), y, 2)


def gather_yx(plan, held):
    _, x, y, _ = plan.bits
    held = in_order(held, plan.over_y(held), y, 1)
    return in_order(held, plan.over_x(held), x, 1)


def scatter_bit(array, bit, axis, move):
    theirs = move(pick(array, 1 - bit, axis))
    return pick(array, bit, axis).astype(F32) + theirs.astype(F32)


def scatter_xy(plan, parts):
    _, x, y, _ = plan.bits
    parts = scatter_bit(parts, x, 1, plan.over_x).astype(BF)
    return scatter_bit(parts, y, 1, plan.over_y).astype(BF)


def scatter_yx(plan, parts):
    _, x, y, _ = plan.bits
    parts = scatter_bit(parts, y, 2, plan.over_y).astype(BF)
    return scatter_bit(parts, x, 1, plan.over_x).astype(BF)


def scatter_z(plan, parts):
    z = plan.bits[0]
    total = pick(parts, z, 0).astype(F32)
    for step in (1, 2, 3):
        total = total + plan.over_z(pick(parts, (z + step) % 4, 0), step).astype(F32)
    return total


def gather_gains(plan, gains):
    if not plan.fast:
        return lax.all_gather(gains, AXES, axis=1, tiled=True)
    z, x, y, core = plan.bits
    held = gather_z(plan, gains)
    held = in_order(held, plan.over_x(held), x, 1)
    held = in_order(held, plan.over_y(held), y, 2)
    held = in_order(held, plan.over_core(held), core, 3)
    return jnp.moveaxis(held, 4, 0).reshape(2, -1)


def scatter_gain(plan, grad):
    if not plan.fast:
        return lax.psum_scatter(grad, AXES, scatter_dimension=0, tiled=True)
    z, x, y, core = plan.bits
    parts = grad.reshape(4, 2, 2, 2, -1)
    parts = scatter_bit(parts, core, 3, plan.over_core)
    parts = scatter_bit(parts, x, 1, plan.over_x)
    parts = scatter_bit(parts, y, 1, plan.over_y)
    return scatter_z(plan, parts)


def group_columns(weight, group):
    rows = weight.shape[0]
    span = HEADS // group * HEAD_DIM
    padded = -(-span // LANES) * LANES
    split = weight.reshape(rows, 3, group, span)
    split = jnp.pad(split, ((0, 0), (0, 0), (0, 0), (0, padded - span)))
    split = split.reshape(rows, 3, group, padded // LANES, LANES)
    return jnp.transpose(split, (0, 2, 3, 1, 4)).reshape(rows, group, -1)


def ungroup_columns(weight):
    rows, group, width = weight.shape
    span = HEADS // group * HEAD_DIM
    pairs = width // (3 * LANES)
    split = jnp.transpose(weight.reshape(rows, group, pairs, 3, LANES), (0, 3, 1, 2, 4))
    split = split.reshape(rows, 3, group, pairs * LANES)[..., :span]
    return split.reshape(rows, 3 * HEADS * HEAD_DIM)


def gather_qkv(plan, shard):
    split = group_columns(shard, plan.group)
    if not plan.fast:
        whole = lax.all_gather(split, AXES, axis=0, tiled=True)
        return pick(whole, plan.member, 1)
    core = plan.bits[3]
    mine = pick(split, core, 1)
    other = plan.over_core(pick(split, 1 - core, 1))
    held = gather_z(plan, in_order(mine, other, core, 0))
    first = gather_xy(plan, held[:, 0])
    second = gather_yx(plan, held[:, 1])
    return jnp.stack([first, second], axis=3).reshape(-1, split.shape[2])


def scatter_qkv(plan, grad):
    width = grad.shape[1]
    if not plan.fast:
        spread = jnp.zeros((plan.group,) + grad.shape, BF)
        spread = lax.dynamic_update_index_in_dim(spread, grad.astype(BF), plan.member, 0)
        full = ungroup_columns(jnp.transpose(spread, (1, 0, 2)))
        return lax.psum_scatter(full.astype(F32), AXES, scatter_dimension=0, tiled=True)
    core = plan.bits[3]
    parts = grad.astype(BF).reshape(4, 2, 2, 2, -1, width)
    first = scatter_xy(plan, parts[:, :, :, 0])
    second = scatter_yx(plan, parts[:, :, :, 1])
    total = scatter_z(plan, jnp.stack([first, second], axis=1))
    other = plan.over_core(pick(total, 1 - core, 0))
    return ungroup_columns(in_order(pick(total, core, 0), other, core, 1))


def gather_rest(plan, out_weight, inner_weight, outer_rows):
    if not plan.fast:
        return tuple(
            lax.all_gather(w, AXES, axis=0, tiled=True) for w in (out_weight, inner_weight, outer_rows)
        )
    core = plan.bits[3]
    held = gather_z(plan, jnp.concatenate([out_weight, outer_rows, inner_weight], axis=1))
    cut = out_weight.shape[1] + outer_rows.shape[1]
    sides = gather_xy(plan, held[..., :cut])
    inner = gather_yx(plan, held[..., cut:])
    sides = in_order(sides, plan.over_core(sides), core, 3).reshape(-1, cut)
    inner = in_order(inner, plan.over_core(inner), core, 3).reshape(-1, inner.shape[-1])
    return sides[:, : out_weight.shape[1]], inner, sides[:, out_weight.shape[1] :]


def scatter_rows(plan, grad, route):
    core = plan.bits[3]
    parts = grad.astype(BF).reshape(4, 2, 2, 2, -1, grad.shape[1])
    parts = scatter_bit(parts, core, 3, plan.over_core).astype(BF)
    return route(plan, parts)


def scatter_whole(plan, grad, route):
    if not plan.fast:
        return lax.psum_scatter(grad, AXES, scatter_dimension=0, tiled=True)
    return scatter_z(plan, scatter_rows(plan, grad, route))


def normalize(rows_in):
    row_mean = jnp.mean(rows_in, axis=-1, keepdims=True)
    centered = rows_in - row_mean
    variance = jnp.mean(centered * centered, axis=-1, keepdims=True)
    inv_std = lax.rsqrt(variance + EPS)
    return (centered * inv_std, inv_std)


def norm_back(grad_normed, normed, inv_std, gain):
    scaled = grad_normed * gain
    return inv_std * (
        scaled
        - jnp.mean(scaled, axis=-1, keepdims=True)
        - normed * jnp.mean(scaled * normed, axis=-1, keepdims=True)
    )


def rope_tables(positions):
    lane = jnp.arange(LANES, dtype=jnp.int32)
    exponent = (lane % (HEAD_DIM // 2)).astype(F32) * (2.0 / HEAD_DIM)
    frequency = jnp.power(F32(THETA), -exponent)
    angles = positions.astype(F32)[:, None] * frequency
    sign = jnp.where(lane % HEAD_DIM < HEAD_DIM // 2, -1.0, 1.0)
    return jnp.cos(angles), jnp.sin(angles) * sign


def doc_tags(starts):
    lane = jnp.arange(LANES, dtype=jnp.int32) % HEAD_DIM
    used = lane < 2 * BITS
    bit = (starts[:, None] >> jnp.where(used, lane // 2, 0)) & 1
    odd = lane % 2
    query_on = used & (bit != odd)
    key_on = used & (bit == odd)
    return (
        jnp.where(query_on, FAR, 0.0).astype(BF),
        jnp.where(key_on, 1.0, 0.0).astype(BF),
    )


def shards(
    hidden_in,
    doc_positions,
    attn_gain,
    qkv_weight,
    out_weight,
    mlp_gain,
    inner_weight,
    outer_weight,
    grad_out,
    *,
    sizes,
):
    seqs, local, width = hidden_in.shape
    plan = Plan(*sizes, seqs)
    group, member = plan.group, plan.member
    other_seq = 1 - plan.seq

    def in_group(array):
        return [array] + [plan.shift(array, step) for step in range(1, group)]

    own_hidden, far_hidden = pick(hidden_in, plan.seq, 0), pick(hidden_in, other_seq, 0)
    own_grad, far_grad = pick(grad_out, plan.seq, 0), pick(grad_out, other_seq, 0)
    own_index = plan.ctx_id * local + jnp.arange(local, dtype=jnp.int32)
    marks = jnp.stack([own_index[None, :] - doc_positions, doc_positions], axis=1)
    gains = gather_gains(plan, jnp.stack([attn_gain, mlp_gain])).astype(F32)
    marks_own = jnp.concatenate(
        [pick(marks, plan.seq, 0), plan.swap(pick(marks, other_seq, 0))], axis=1
    )
    rows_in = jnp.concatenate(
        [own_hidden, plan.swap(far_hidden.astype(BF)).astype(F32)], axis=0
    )
    tokens = rows_in.shape[0]
    marks_all = jnp.concatenate(in_group(marks_own), axis=1)
    qkv_columns = gather_qkv(plan, qkv_weight)

    normed_own, inv_one = normalize(rows_in)
    first_own = (normed_own * gains[0]).astype(BF)
    normed_pieces = in_group(normed_own.astype(BF))
    first_in = jnp.concatenate(in_group(first_own), axis=0)
    normed_all = jnp.concatenate([normed_own.astype(BF)] + normed_pieces[1:], axis=0)
    cos_table, sine_table = rope_tables(marks_all[1])
    qtag, ktag = doc_tags(marks_all[0])

    out_full, inner_full, outer_rows = gather_rest(
        plan, out_weight, inner_weight, jnp.transpose(outer_weight)
    )
    grad_rows = jnp.concatenate([own_grad, plan.swap(far_grad.astype(BF)).astype(F32)], axis=0)

    qkv_rows = mm(first_in, qkv_columns)
    kept, context_heads, lse = attend(qkv_rows, cos_table, sine_table, qtag, ktag)

    span = HEADS // group * HEAD_DIM

    def join_heads(pieces):
        if group == 2:
            return jnp.where(
                member == 0,
                jnp.concatenate(pieces, axis=1),
                jnp.concatenate(pieces[::-1], axis=1),
            )
        ring = jnp.concatenate(pieces + pieces, axis=1)
        return lax.dynamic_slice_in_dim(ring, (group - member) % group * span, group * span, 1)

    mine = context_heads[:, :span]
    context_b = join_heads(
        [mine[:tokens]]
        + [
            plan.shift(mine[step * tokens : (step + 1) * tokens], -step)
            for step in range(1, group)
        ]
    )
    attn_part = mm(context_b, out_full)
    middle = rows_in + attn_part
    normed_two, inv_two = normalize(middle)
    second_in = (normed_two * gains[1]).astype(BF)
    gate_up = mm(second_in, inner_full)
    gate, up = gate_up[:, :FF], gate_up[:, FF:]
    below = 0.5 * (1.0 + lax.erf(gate * math.sqrt(0.5)))
    bell = jnp.exp(-0.5 * gate * gate) * (1.0 / math.sqrt(2.0 * math.pi))
    gelu = gate * below
    gated = (gelu * up).astype(BF)
    added = attn_part + mm(gated, outer_rows, NT)
    output_own = own_hidden + added[:local]
    output_far = far_hidden + plan.swap(added[local:].astype(BF)).astype(F32)

    branch_b = grad_rows.astype(BF)
    gated_grad = mm(branch_b, outer_rows)
    gate_up_grad = jnp.concatenate(
        [gated_grad * up * (below + gate * bell), gated_grad * gelu], axis=1
    ).astype(BF)
    second_grad = mm(gate_up_grad, inner_full, NT)
    mlp_gain_grad = scatter_gain(plan, jnp.sum(second_grad * normed_two, axis=0))
    middle_part = norm_back(second_grad, normed_two, inv_two, gains[1])
    attn_b = (grad_rows + middle_part).astype(BF)
    context_grad = mm(attn_b, out_full, NT).astype(BF)

    outer_grad = scatter_whole(plan, mm(branch_b, gated, TN), scatter_yx)
    inner_grad = scatter_whole(plan, mm(second_in, gate_up_grad, TN), scatter_xy)
    out_grad = scatter_whole(plan, mm(context_b, attn_b, TN), scatter_yx)

    split_grad = context_grad.reshape(tokens, group, span)
    grad_pieces = [pick(split_grad, member, 1)] + [
        plan.shift(pick(split_grad, (member + step) % group, 1), step) for step in range(1, group)
    ]
    heads_grad = jnp.concatenate(grad_pieces, axis=0)
    heads_grad = jnp.pad(heads_grad, ((0, 0), (0, context_heads.shape[1] - span)))
    qkv_grad = attend_back(
        kept, context_heads, heads_grad, lse, cos_table, sine_table, qtag, ktag
    )
    qkv_weight_grad = scatter_qkv(plan, mm(first_in, qkv_grad, TN))
    first_part = mm(qkv_grad, qkv_columns, NT)
    attn_gain_grad = scatter_gain(plan, jnp.sum(first_part * normed_all.astype(F32), axis=0))
    first_grad = first_part[:tokens]
    for step in range(1, group):
        piece = first_part[step * tokens : (step + 1) * tokens].astype(BF)
        first_grad = first_grad + plan.shift(piece, -step).astype(F32)
    grad_added = middle_part + norm_back(first_grad, normed_own, inv_one, gains[0])
    input_own = own_grad + grad_added[:local]
    input_far = far_grad + plan.swap(grad_added[local:].astype(BF)).astype(F32)

    return (
        in_order(output_own, output_far, plan.seq, 0),
        in_order(input_own, input_far, plan.seq, 0),
        attn_gain_grad,
        qkv_weight_grad,
        out_grad,
        mlp_gain_grad,
        inner_grad,
        jnp.transpose(outer_grad),
    )


def solution(mesh):
    sizes = (mesh.shape["dp"], mesh.shape["ctx"])
    return jax.shard_map(
        functools.partial(shards, sizes=sizes),
        mesh=mesh,
        in_specs=(
            P("dp", "ctx", None),
            P("dp", "ctx"),
            P(AXES),
            P(AXES, None),
            P(AXES, None),
            P(AXES),
            P(AXES, None),
            P(None, AXES),
            P("dp", "ctx", None),
        ),
        out_specs=(
            P("dp", "ctx", None),
            P("dp", "ctx", None),
            P(AXES),
            P(AXES, None),
            P(AXES, None),
            P(AXES),
            P(AXES, None),
            P(None, AXES),
        ),
        check_vma=False,
    )
```

```python
import functools
import math

import jax
import jax.numpy as jnp
from jax import lax
from jax.experimental import pallas as pl
from jax.experimental.pallas import tpu as pltpu
from jax.sharding import PartitionSpec as P

HEADS = 12
HEAD_DIM = 64
FF = 1152
LANES = 128

EPS = 1e-05
THETA = 160000.0
FAR = -(2.0**99)
BITS = 16

AXES = ("dp", "ctx")
BF = jnp.bfloat16
F32 = jnp.float32

NT = (((1,), (1,)), ((), ()))
TN = (((0,), (0,)), ((), ()))
NN = (((1,), (0,)), ((), ()))


def mm(lhs, rhs, dims=NN):
    return lax.dot_general(lhs, rhs, dims, preferred_element_type=F32)


def turn(rows, cos_table, sine_table, front):
    ahead = pltpu.roll(rows, LANES - HEAD_DIM // 2, 1)
    behind = pltpu.roll(rows, HEAD_DIM // 2, 1)
    return rows * cos_table, jnp.where(front, ahead, behind) * sine_table


def lane_masks(rows):
    lane = lax.broadcasted_iota(jnp.int32, (rows, LANES), 1)
    return lane < HEAD_DIM, (lane % HEAD_DIM) < HEAD_DIM // 2


def attend_kernel(block, qkv_ref, cos_ref, sin_ref, qtag_ref, ktag_ref, kept_ref, ctx_ref, lse_ref):
    length = qkv_ref.shape[0]
    low, front = lane_masks(length)
    cos_table, sine_table = cos_ref[...], sin_ref[...]
    plain, crossed = turn(qkv_ref[:, :LANES], cos_table, sine_table, front)
    kept_ref[:, :LANES] = ((plain + crossed) * (1.0 / math.sqrt(HEAD_DIM))).astype(BF)
    plain, crossed = turn(qkv_ref[:, LANES : 2 * LANES], cos_table, sine_table, front)
    keys = (plain + crossed).astype(BF)
    kept_ref[:, LANES : 2 * LANES] = keys
    values = qkv_ref[:, 2 * LANES :].astype(BF)
    kept_ref[:, 2 * LANES :] = values
    values = values.astype(F32)
    ktag = ktag_ref[...]
    low_rows = lax.broadcasted_iota(jnp.int32, (LANES, block), 0) < HEAD_DIM
    low_block = low[:block]
    keys_of = (jnp.where(low, keys, ktag), jnp.where(low, ktag, keys))
    values_of = (
        jnp.transpose(jnp.where(low, values, 1.0)).astype(BF),
        jnp.transpose(jnp.where(low, 1.0, values)).astype(BF),
    )
    for start in range(0, length, block):
        queries = kept_ref[start : start + block, :LANES]
        qtag = qtag_ref[start : start + block, :]
        queries_of = (jnp.where(low_block, queries, qtag), jnp.where(low_block, qtag, queries))
        parts = []
        for head in range(2):
            scores = mm(keys_of[head], queries_of[head], NT)
            top = jnp.max(scores, axis=0, keepdims=True)
            terms = jnp.exp(scores - top).astype(BF)
            mixed = mm(values_of[head], terms)
            total = mixed[HEAD_DIM : HEAD_DIM + 1] if head == 0 else mixed[:1]
            lse_ref[0, head : head + 1, start : start + block] = top + jnp.log(total)
            parts.append(mixed / total)
        joined = jnp.where(low_rows, parts[0], parts[1])
        ctx_ref[start : start + block, :] = jnp.transpose(joined).astype(BF)


def attend_back_kernel(
    block, kept_ref, ctx_ref, grad_ref, lse_ref, cos_ref, sin_ref, qtag_ref, ktag_ref, out_ref, acc_ref
):
    length = kept_ref.shape[0]
    low, front = lane_masks(length)
    zero = jnp.zeros((length, LANES), BF)
    queries = kept_ref[:, :LANES]
    grads = grad_ref[...]
    qtag = qtag_ref[...]
    queries_of = (jnp.where(low, queries, qtag), jnp.where(low, qtag, queries))
    clean_of = (jnp.where(low, queries, zero), jnp.where(low, zero, queries))
    grads_of = (jnp.where(low, grads, zero), jnp.where(low, zero, grads))
    product = jnp.transpose(grads.astype(F32) * ctx_ref[...].astype(F32))
    delta_of = (
        jnp.sum(product[:HEAD_DIM], axis=0, keepdims=True),
        jnp.sum(product[HEAD_DIM:], axis=0, keepdims=True),
    )
    low_block = low[:block]
    zero_block = zero[:block]
    for start in range(0, length, block):
        rows = slice(start, start + block)
        keys = kept_ref[rows, LANES : 2 * LANES]
        values = kept_ref[rows, 2 * LANES :]
        ktag = ktag_ref[rows, :]
        keys_of = (jnp.where(low_block, keys, ktag), jnp.where(low_block, ktag, keys))
        keys_f = keys.astype(F32)
        key_grad = value_grad = query_part = None
        for head in range(2):
            scores = mm(keys_of[head], queries_of[head], NT)
            probs = jnp.exp(scores - lse_ref[0, head : head + 1, :])
            prob_grad = mm(values, grads_of[head], NT)
            score_grad = (probs * (prob_grad - delta_of[head])).astype(BF)
            value_term = mm(probs.astype(BF), grads_of[head])
            key_term = mm(score_grad, clean_of[head])
            mine = low_block if head == 0 else jnp.logical_not(low_block)
            turned = jnp.transpose(jnp.where(mine, keys_f, 0.0)).astype(BF)
            query_term = mm(turned, score_grad)
            value_grad = value_term if head == 0 else value_grad + value_term
            key_grad = key_term if head == 0 else key_grad + key_term
            query_part = query_term if head == 0 else query_part + query_term
        acc_ref[...] = query_part if start == 0 else acc_ref[...] + query_part
        plain, crossed = turn(key_grad, cos_ref[rows, :], sin_ref[rows, :], front[:block])
        out_ref[rows, LANES : 2 * LANES] = (plain - crossed).astype(BF)
        out_ref[rows, 2 * LANES :] = value_grad.astype(BF)
    query_grad = jnp.transpose(acc_ref[...]) * (1.0 / math.sqrt(HEAD_DIM))
    plain, crossed = turn(query_grad, cos_ref[...], sin_ref[...], front)
    out_ref[:, :LANES] = (plain - crossed).astype(BF)


def whole_block(length):
    return pl.BlockSpec((length, LANES), lambda j: (0, 0))


def column_block(length, width):
    return pl.BlockSpec((length, width), lambda j: (0, 0))


def attend(qkv_rows, cos_table, sine_table, qtag, ktag):
    length = qkv_rows.shape[0]
    return pl.pallas_call(
        functools.partial(attend_kernel, 256),
        grid=(1,),
        in_specs=[column_block(length, 3 * LANES)] + [whole_block(length)] * 4,
        out_specs=[
            column_block(length, 3 * LANES),
            column_block(length, LANES),
            pl.BlockSpec((1, 2, length), lambda j: (0, 0, 0)),
        ],
        out_shape=[
            jax.ShapeDtypeStruct((length, 3 * LANES), BF),
            jax.ShapeDtypeStruct((length, LANES), BF),
            jax.ShapeDtypeStruct((1, 2, length), F32),
        ],
        compiler_params=pltpu.CompilerParams(vmem_limit_bytes=48 * 1024 * 1024),
        cost_estimate=pl.CostEstimate(
            flops=2 * 2 * 2 * length * length * 512,
            bytes_accessed=length * LANES * 20,
            transcendentals=2 * length * length,
        ),
    )(qkv_rows, cos_table, sine_table, qtag, ktag)


def attend_back(kept, context, context_grad, lse, cos_table, sine_table, qtag, ktag):
    length = kept.shape[0]
    return pl.pallas_call(
        functools.partial(attend_back_kernel, 256),
        grid=(1,),
        in_specs=[
            column_block(length, 3 * LANES),
            column_block(length, LANES),
            column_block(length, LANES),
            pl.BlockSpec((1, 2, length), lambda j: (0, 0, 0)),
        ]
        + [whole_block(length)] * 4,
        out_specs=column_block(length, 3 * LANES),
        out_shape=jax.ShapeDtypeStruct((length, 3 * LANES), BF),
        scratch_shapes=[pltpu.VMEM((LANES, length), F32)],
        compiler_params=pltpu.CompilerParams(vmem_limit_bytes=48 * 1024 * 1024),
        cost_estimate=pl.CostEstimate(
            flops=2 * 5 * 2 * length * length * 256,
            bytes_accessed=length * LANES * 20,
            transcendentals=2 * length * length,
        ),
    )(kept, context, context_grad, lse, cos_table, sine_table, qtag, ktag)


class Plan:
    def __init__(self, dp, ctx, seqs):
        self.dp, self.ctx = dp, ctx
        self.group = ctx // seqs
        self.fast = (dp, ctx, self.group) == (8, 4, 2)
        self.ctx_id = lax.axis_index("ctx")
        self.dp_id = lax.axis_index("dp")
        self.member = self.ctx_id % self.group
        self.seq = self.ctx_id // self.group

    def permute(self, array, target):
        pairs = []
        for dp in range(self.dp):
            for ctx in range(self.ctx):
                far_dp, far_ctx = target(dp, ctx)
                pairs.append((dp * self.ctx + ctx, far_dp * self.ctx + far_ctx))
        return lax.ppermute(array, AXES, pairs)

    def swap(self, array):
        return self.permute(array, lambda dp, ctx: (dp, (ctx + self.group) % self.ctx))

    def shift(self, array, step):
        size = self.group
        return self.permute(
            array, lambda dp, ctx: (dp, ctx // size * size + (ctx % size + step) % size)
        )

    def bit(self, name):
        if name in ("y", "core"):
            return self.ctx_id // 2 if name == "y" else self.ctx_id % 2
        return self.dp_id // {"zh": 4, "zl": 2, "x": 1}[name] % 2

    def cross(self, array, name):
        flip_dp = {"zh": 4, "zl": 2, "x": 1}.get(name, 0)
        flip_ctx = {"y": 2, "core": 1}.get(name, 0)
        return self.permute(array, lambda dp, ctx: (dp ^ flip_dp, ctx ^ flip_ctx))


ORDER = ("zh", "zl", "x", "y", "core")
ROUTES = (("zl", "x", "y"), ("x", "y", "zl"), ("y", "zl", "x"))


def in_order(mine, other, bit, axis):
    return jnp.where(
        bit == 0, jnp.stack([mine, other], axis=axis), jnp.stack([other, mine], axis=axis)
    )


def pick(array, index, axis):
    return lax.dynamic_index_in_dim(array, index, axis, keepdims=False)


def tie(*arrays):
    return lax.optimization_barrier(arrays)


class Pieces:
    def __init__(self, plan, array, bits):
        self.plan, self.array, self.bits = plan, array, bits

    def grow(self, name):
        bits = [b for b in ORDER if b in self.bits or b == name]
        theirs = self.plan.cross(self.array, name)
        return Pieces(
            self.plan,
            in_order(self.array, theirs, self.plan.bit(name), bits.index(name)),
            bits,
        )

    def shrink(self, name, last=False):
        axis, bit = self.bits.index(name), self.plan.bit(name)
        theirs = self.plan.cross(pick(self.array, 1 - bit, axis), name)
        total = pick(self.array, bit, axis).astype(F32) + theirs.astype(F32)
        return Pieces(
            self.plan, total if last else total.astype(BF), [b for b in self.bits if b != name]
        )

    def rows(self):
        return self.array.reshape(-1, self.array.shape[-1])


def tie_pieces(array, routes):
    array, *held = tie(array, *[route.array for route in routes])
    return array, [Pieces(r.plan, h, r.bits) for r, h in zip(routes, held)]


def by_owner(plan, grad):
    return Pieces(plan, grad.reshape(2, 2, 2, 2, 2, -1, grad.shape[-1]), list(ORDER))


def group_columns(weight, group):
    rows = weight.shape[0]
    span = HEADS // group * HEAD_DIM
    padded = -(-span // LANES) * LANES
    split = weight.reshape(rows, 3, group, span)
    split = jnp.pad(split, ((0, 0), (0, 0), (0, 0), (0, padded - span)))
    split = split.reshape(rows, 3, group, padded // LANES, LANES)
    return jnp.transpose(split, (0, 2, 3, 1, 4)).reshape(rows, group, -1)


def ungroup_columns(weight):
    rows, group, width = weight.shape
    span = HEADS // group * HEAD_DIM
    pairs = width // (3 * LANES)
    split = jnp.transpose(weight.reshape(rows, group, pairs, 3, LANES), (0, 3, 1, 2, 4))
    split = split.reshape(rows, 3, group, pairs * LANES)[..., :span]
    return split.reshape(rows, 3 * HEADS * HEAD_DIM)


def own_rows(plan, grad, core):
    return pick(grad.reshape(2, 2, 2, 2, 2, -1, grad.shape[-1]), core, 4)


def scatter_all(grad):
    return lax.psum_scatter(grad.astype(F32), AXES, scatter_dimension=0, tiled=True)


def scatter_columns_all(plan, grad):
    spread = jnp.zeros((plan.group,) + grad.shape, F32)
    spread = lax.dynamic_update_index_in_dim(spread, grad.astype(F32), plan.member, 0)
    return scatter_all(ungroup_columns(jnp.transpose(spread, (1, 0, 2))))


def normalize(rows_in):
    row_mean = jnp.mean(rows_in, axis=-1, keepdims=True)
    centered = rows_in - row_mean
    variance = jnp.mean(centered * centered, axis=-1, keepdims=True)
    inv_std = lax.rsqrt(variance + EPS)
    return (centered * inv_std, inv_std)


def norm_back(scaled, normed, inv_std):
    return inv_std * (
        scaled
        - jnp.mean(scaled, axis=-1, keepdims=True)
        - normed * jnp.mean(scaled * normed, axis=-1, keepdims=True)
    )


def rope_tables(positions):
    lane = jnp.arange(LANES, dtype=jnp.int32)
    exponent = (lane % (HEAD_DIM // 2)).astype(F32) * (2.0 / HEAD_DIM)
    frequency = jnp.power(F32(THETA), -exponent)
    angles = positions.astype(F32)[:, None] * frequency
    sign = jnp.where(lane % HEAD_DIM < HEAD_DIM // 2, -1.0, 1.0)
    return jnp.cos(angles), jnp.sin(angles) * sign


def doc_tags(starts):
    lane = jnp.arange(LANES, dtype=jnp.int32) % HEAD_DIM
    used = lane < 2 * BITS
    bit = (starts[:, None] >> jnp.where(used, lane // 2, 0)) & 1
    odd = lane % 2
    query_on = used & (bit != odd)
    key_on = used & (bit == odd)
    return (
        jnp.where(query_on, FAR, 0.0).astype(BF),
        jnp.where(key_on, 1.0, 0.0).astype(BF),
    )


def shards(
    hidden_in,
    doc_positions,
    attn_gain,
    qkv_weight,
    out_weight,
    mlp_gain,
    inner_weight,
    outer_weight,
    grad_out,
    *,
    sizes,
):
    seqs, local, width = hidden_in.shape
    plan = Plan(*sizes, seqs)
    group, member = plan.group, plan.member
    other_seq = 1 - plan.seq

    def in_group(array):
        return [array] + [plan.shift(array, step) for step in range(1, group)]

    def pack(positions):
        rows = [
            jnp.concatenate([p // 256, p % 256, jnp.zeros(width - 2 * local, jnp.int32)])
            for p in positions
        ]
        return jnp.pad(jnp.stack(rows), ((0, 16 - len(rows)), (0, 0))).astype(BF)

    def unpack(rows):
        whole = rows.astype(jnp.int32)
        return whole[:local] * 256 + whole[local : 2 * local]

    own_hidden, far_hidden = pick(hidden_in, plan.seq, 0), pick(hidden_in, other_seq, 0)
    own_grad, far_grad = pick(grad_out, plan.seq, 0), pick(grad_out, other_seq, 0)
    own_marks, far_marks = pick(doc_positions, plan.seq, 0), pick(doc_positions, other_seq, 0)
    far_rows = jnp.concatenate(
        [far_hidden.astype(BF), far_grad.astype(BF), pack([far_marks])], axis=0
    )

    gain_one, gain_two = attn_gain.astype(F32)[:, None], mlp_gain.astype(F32)[:, None]
    qkv_scaled = (qkv_weight.astype(F32) * gain_one).astype(BF)
    inner_scaled = (inner_weight.astype(F32) * gain_two).astype(BF)
    outer_shard = jnp.transpose(outer_weight)
    split = group_columns(qkv_scaled, group)
    pairs = split.shape[2] // (3 * LANES)
    pair_columns = [slice(at * 3 * LANES, (at + 1) * 3 * LANES) for at in range(pairs)]
    if plan.fast:
        core = plan.bit("core")
        there, far_rows = tie(pick(split, 1 - core, 1), far_rows)
        there = plan.cross(there, "core")
        held = Pieces(plan, in_order(pick(split, core, 1), there, core, 0), ["core"]).grow("zh")
        cuts = (0, 640, 896, FF)
        outer_cuts = [outer_shard[:, cuts[at] : cuts[at + 1]] for at in range(3)]
        rest = jnp.concatenate(
            [out_weight, outer_cuts[0], inner_scaled[:, :FF], outer_cuts[1]]
            + [inner_scaled[:, FF:], outer_cuts[2]],
            axis=1,
        )
        rest, (held,) = tie_pieces(rest, [held])
        rest = Pieces(plan, rest, []).grow("zh")
        routes = [Pieces(plan, held.array[..., columns], held.bits) for columns in pair_columns]
        for stage in range(2):
            routes = [r.grow(ROUTES[at][stage]) for at, r in enumerate(routes)]
        rest_whole, routes = tie_pieces(rest.array, routes)
        routes = [r.grow(ROUTES[at][2]) for at, r in enumerate(routes)]
        third = rest_whole.shape[-1] // 3
        rest = [
            Pieces(plan, rest_whole[..., at * third : (at + 1) * third], rest.bits)
            for at in range(3)
        ]
        rest = [r.grow(ROUTES[at][0]) for at, r in enumerate(rest)]
        qkv_columns = [r.rows() for r in routes]
    else:
        whole = pick(lax.all_gather(split, AXES, axis=0, tiled=True), member, 1)
        qkv_columns = [whole[:, columns] for columns in pair_columns]

    swapped = plan.swap(far_rows)
    rows_in = jnp.concatenate([own_hidden, swapped[:local].astype(F32)], axis=0)
    grad_rows = jnp.concatenate([own_grad, swapped[local : 2 * local].astype(F32)], axis=0)
    tokens = rows_in.shape[0]
    marks_own = [own_marks, unpack(swapped[2 * local])]
    normed_one, inv_one = normalize(rows_in)
    shared = in_group(jnp.concatenate([normed_one.astype(BF), pack(marks_own)], axis=0))
    first_in = jnp.concatenate([piece[:tokens] for piece in shared], axis=0)
    positions, starts = [], []
    for step, piece in enumerate(shared):
        marks = marks_own if step == 0 else [unpack(piece[tokens]), unpack(piece[tokens + 1])]
        block = plan.seq * group + (member - step) % group
        for at, mark in enumerate(marks):
            index = (block + at * group) % plan.ctx * local + jnp.arange(local, dtype=jnp.int32)
            positions.append(mark)
            starts.append(index - mark)
    cos_table, sine_table = rope_tables(jnp.concatenate(positions))
    qtag, ktag = doc_tags(jnp.concatenate(starts))

    attended = []
    for pair in range(pairs):
        qkv_rows = mm(first_in, qkv_columns[pair])
        if pair < 2 and plan.fast:
            qkv_rows, rest = tie_pieces(qkv_rows, rest)
            rest = [r.grow(ROUTES[at][pair + 1]) for at, r in enumerate(rest)]
        attended.append(attend(qkv_rows, cos_table, sine_table, qtag, ktag))

    span = HEADS // group * HEAD_DIM

    def join_heads(pieces):
        if group == 2:
            return jnp.where(
                member == 0,
                jnp.concatenate(pieces, axis=1),
                jnp.concatenate(pieces[::-1], axis=1),
            )
        ring = jnp.concatenate(pieces + pieces, axis=1)
        return lax.dynamic_slice_in_dim(ring, (group - member) % group * span, group * span, 1)

    def heads_of(array, index):
        pieces = [array[:, at * span : (at + 1) * span] for at in range(group)]
        chosen = pieces[0]
        for at in range(1, group):
            chosen = jnp.where(index == at, pieces[at], chosen)
        return chosen

    def context_rows(step):
        rows = slice(step * tokens, (step + 1) * tokens)
        return jnp.concatenate([context[rows] for _, context, _ in attended], axis=1)[:, :span]

    context_b = join_heads(
        [context_rows(0)] + [plan.shift(context_rows(step), -step) for step in range(1, group)]
    )
    if plan.fast:
        rest = [r.grow("core").rows() for r in rest]
        heads_width = HEADS * HEAD_DIM
        out_full, inner_gate, inner_up = rest[0][:, :heads_width], rest[1][:, :FF], rest[2][:, :FF]
        outer_rows = jnp.concatenate(
            [rest[0][:, heads_width:], rest[1][:, FF:], rest[2][:, FF:]], axis=1
        )
    else:
        out_full, outer_rows, inner_full = (
            lax.all_gather(w, AXES, axis=0, tiled=True)
            for w in (out_weight, outer_shard, inner_scaled)
        )
        inner_gate, inner_up = inner_full[:, :FF], inner_full[:, FF:]
    attn_part = mm(context_b, out_full)
    middle = rows_in + attn_part
    normed_two, inv_two = normalize(middle)
    second_in = normed_two.astype(BF)
    gate, up = mm(second_in, inner_gate), mm(second_in, inner_up)
    below = 0.5 * (1.0 + lax.erf(gate * math.sqrt(0.5)))
    bell = jnp.exp(-0.5 * gate * gate) * (1.0 / math.sqrt(2.0 * math.pi))
    gelu = gate * below
    gated = (gelu * up).astype(BF)
    branch_b = grad_rows.astype(BF)
    outer_grad = mm(branch_b, gated, TN).astype(BF)
    added = attn_part + mm(gated, outer_rows, NT)
    output_own = own_hidden + added[:local]
    output_far = far_hidden + plan.swap(added[local:].astype(BF)).astype(F32)

    gated_grad = mm(branch_b, outer_rows)
    gate_grad = (gated_grad * up * (below + gate * bell)).astype(BF)
    up_grad = (gated_grad * gelu).astype(BF)
    inner_grad = [mm(second_in, gate_grad, TN).astype(BF), mm(second_in, up_grad, TN).astype(BF)]
    if plan.fast:
        mlp_routes = [by_owner(plan, g).shrink("core") for g in [outer_grad] + inner_grad]
    second_grad = mm(gate_grad, inner_gate, NT) + mm(up_grad, inner_up, NT)
    middle_part = norm_back(second_grad, normed_two, inv_two)
    attn_b = (grad_rows + middle_part).astype(BF)
    context_grad = mm(attn_b, out_full, NT).astype(BF)
    grad_pieces = [heads_of(context_grad, member)] + [
        plan.shift(heads_of(context_grad, (member + step) % group), step)
        for step in range(1, group)
    ]
    heads_grad = jnp.concatenate(grad_pieces, axis=0)
    heads_grad = jnp.pad(heads_grad, ((0, 0), (0, pairs * LANES - span)))
    out_grad = mm(context_b, attn_b, TN).astype(BF)
    if plan.fast:
        heads_grad, mlp_routes = tie_pieces(heads_grad, mlp_routes)
        mlp_routes = [r.shrink(ROUTES[at][2]) for at, r in enumerate(mlp_routes)]
        out_grad = by_owner(plan, out_grad).shrink("core").array
        third = out_grad.shape[-1] // 3
        attn_routes = []

    qkv_grads, qkv_weight_grads = [], []
    for pair in range(pairs):
        kept, context, lse = attended[pair]
        pair_grad = heads_grad[:, pair * LANES : (pair + 1) * LANES]
        if pair > 0 and plan.fast:
            pair_grad, mlp_routes = tie_pieces(pair_grad, mlp_routes)
            mlp_routes = [r.shrink(ROUTES[at][2 - pair]) for at, r in enumerate(mlp_routes)]
        qkv_grads.append(
            attend_back(kept, context, pair_grad, lse, cos_table, sine_table, qtag, ktag)
        )
        grad = mm(first_in, qkv_grads[pair], TN).astype(BF)
        qkv_weight_grads.append(grad)
        if plan.fast:
            if pair == 2:
                grad, mlp_routes = tie_pieces(grad, mlp_routes)
            parts = [out_grad[..., pair * third : (pair + 1) * third]]
            parts += [own_rows(plan, grad, core) for core in (0, 1)]
            route = Pieces(plan, jnp.concatenate(parts, axis=-1), list(ORDER[:4]))
            attn_routes.append(route.shrink(ROUTES[pair][2]))
    if plan.fast:
        mlp_whole = Pieces(
            plan, jnp.concatenate([r.array for r in mlp_routes], axis=-1), ["zh"]
        ).shrink("zh", last=True)
        attn_routes = [r.shrink(ROUTES[at][1]) for at, r in enumerate(attn_routes)]
        attn_routes = [r.shrink(ROUTES[at][0]) for at, r in enumerate(attn_routes)]
        attn_sum = Pieces(
            plan, jnp.concatenate([r.array for r in attn_routes], axis=-1), ["zh"]
        ).shrink("zh", last=True).array.reshape(-1, pairs, attn_routes[0].array.shape[-1])
        out_sum = attn_sum[..., :third].reshape(-1, 3 * third)
        qkv_sum = attn_sum[..., third:].reshape(-1, pairs, 2, 3 * LANES)
        core = plan.bit("core")
        other = plan.cross(pick(qkv_sum, 1 - core, 2), "core")
        qkv_sum = in_order(pick(qkv_sum, core, 2), other, core, 1)
        qkv_sum = ungroup_columns(qkv_sum.reshape(-1, 2, pairs * 3 * LANES))
        outer_sum, inner_sum = mlp_whole.array[:, :FF], mlp_whole.array[:, FF:]
    else:
        out_sum, outer_sum = scatter_all(out_grad), scatter_all(outer_grad)
        inner_sum = scatter_all(jnp.concatenate(inner_grad, axis=1))
        qkv_sum = scatter_columns_all(plan, jnp.concatenate(qkv_weight_grads, axis=1))
    first_part = mm(
        jnp.concatenate(qkv_grads, axis=1), jnp.concatenate(qkv_columns, axis=1), NT
    )
    first_grad = first_part[:tokens]
    for step in range(1, group):
        piece = first_part[step * tokens : (step + 1) * tokens].astype(BF)
        first_grad = first_grad + plan.shift(piece, -step).astype(F32)
    grad_added = middle_part + norm_back(first_grad, normed_one, inv_one)
    input_own = own_grad + grad_added[:local]
    input_far = far_grad + plan.swap(grad_added[local:].astype(BF)).astype(F32)

    return (
        in_order(output_own, output_far, plan.seq, 0),
        in_order(input_own, input_far, plan.seq, 0),
        jnp.sum(qkv_sum * qkv_weight.astype(F32), axis=1),
        qkv_sum * gain_one,
        out_sum,
        jnp.sum(inner_sum * inner_weight.astype(F32), axis=1),
        inner_sum * gain_two,
        jnp.transpose(outer_sum),
    )


def solution(mesh):
    sizes = (mesh.shape["dp"], mesh.shape["ctx"])
    return jax.shard_map(
        functools.partial(shards, sizes=sizes),
        mesh=mesh,
        in_specs=(
            P("dp", "ctx", None),
            P("dp", "ctx"),
            P(AXES),
            P(AXES, None),
            P(AXES, None),
            P(AXES),
            P(AXES, None),
            P(None, AXES),
            P("dp", "ctx", None),
        ),
        out_specs=(
            P("dp", "ctx", None),
            P("dp", "ctx", None),
            P(AXES),
            P(AXES, None),
            P(AXES, None),
            P(AXES),
            P(AXES, None),
            P(None, AXES),
        ),
        check_vma=False,
    )
```

```python
import functools
import math

import jax
import jax.numpy as jnp
from jax import lax
from jax.experimental import pallas as pl
from jax.experimental.pallas import tpu as pltpu
from jax.sharding import PartitionSpec as P

HEADS = 12
HEAD_DIM = 64
FF = 1152
LANES = 128

EPS = 1e-05
THETA = 160000.0
FAR = -(2.0**99)
BITS = 16

AXES = ("dp", "ctx")
BF = jnp.bfloat16
F32 = jnp.float32

NT = (((1,), (1,)), ((), ()))
TN = (((0,), (0,)), ((), ()))
NN = (((1,), (0,)), ((), ()))


def mm(lhs, rhs, dims=NN):
    return lax.dot_general(lhs, rhs, dims, preferred_element_type=F32)


def turn(rows, cos_table, sine_table, front):
    ahead = pltpu.roll(rows, LANES - HEAD_DIM // 2, 1)
    behind = pltpu.roll(rows, HEAD_DIM // 2, 1)
    return rows * cos_table, jnp.where(front, ahead, behind) * sine_table


def lane_masks(rows):
    lane = lax.broadcasted_iota(jnp.int32, (rows, LANES), 1)
    return lane < HEAD_DIM, (lane % HEAD_DIM) < HEAD_DIM // 2


def attend_kernel(block, qkv_ref, cos_ref, sin_ref, qtag_ref, ktag_ref, kept_ref, ctx_ref, lse_ref):
    length = qkv_ref.shape[0]
    low, front = lane_masks(length)
    cos_table, sine_table = cos_ref[...], sin_ref[...]
    plain, crossed = turn(qkv_ref[:, :LANES], cos_table, sine_table, front)
    kept_ref[:, :LANES] = ((plain + crossed) * (1.0 / math.sqrt(HEAD_DIM))).astype(BF)
    plain, crossed = turn(qkv_ref[:, LANES : 2 * LANES], cos_table, sine_table, front)
    keys = (plain + crossed).astype(BF)
    kept_ref[:, LANES : 2 * LANES] = keys
    values = qkv_ref[:, 2 * LANES :].astype(BF)
    kept_ref[:, 2 * LANES :] = values
    values = values.astype(F32)
    ktag = ktag_ref[...]
    low_rows = lax.broadcasted_iota(jnp.int32, (LANES, block), 0) < HEAD_DIM
    low_block = low[:block]
    keys_of = (jnp.where(low, keys, ktag), jnp.where(low, ktag, keys))
    values_of = (
        jnp.transpose(jnp.where(low, values, 1.0)).astype(BF),
        jnp.transpose(jnp.where(low, 1.0, values)).astype(BF),
    )
    for start in range(0, length, block):
        queries = kept_ref[start : start + block, :LANES]
        qtag = qtag_ref[start : start + block, :]
        queries_of = (jnp.where(low_block, queries, qtag), jnp.where(low_block, qtag, queries))
        parts = []
        for head in range(2):
            scores = mm(keys_of[head], queries_of[head], NT)
            top = jnp.max(scores, axis=0, keepdims=True)
            terms = jnp.exp(scores - top).astype(BF)
            mixed = mm(values_of[head], terms)
            total = mixed[HEAD_DIM : HEAD_DIM + 1] if head == 0 else mixed[:1]
            lse_ref[head : head + 1, start : start + block] = top + jnp.log(total)
            parts.append(mixed / total)
        joined = jnp.where(low_rows, parts[0], parts[1])
        ctx_ref[start : start + block, :] = jnp.transpose(joined).astype(BF)


def attend_back_kernel(
    block, kept_ref, ctx_ref, grad_ref, lse_ref, cos_ref, sin_ref, qtag_ref, ktag_ref, out_ref, acc_ref
):
    length = kept_ref.shape[0]
    low, front = lane_masks(length)
    zero = jnp.zeros((length, LANES), BF)
    queries = kept_ref[:, :LANES]
    grads = grad_ref[...]
    qtag = qtag_ref[...]
    queries_of = (jnp.where(low, queries, qtag), jnp.where(low, qtag, queries))
    clean_of = (jnp.where(low, queries, zero), jnp.where(low, zero, queries))
    grads_of = (jnp.where(low, grads, zero), jnp.where(low, zero, grads))
    product = jnp.transpose(grads.astype(F32) * ctx_ref[...].astype(F32))
    delta_of = (
        jnp.sum(product[:HEAD_DIM], axis=0, keepdims=True),
        jnp.sum(product[HEAD_DIM:], axis=0, keepdims=True),
    )
    low_block = low[:block]
    zero_block = zero[:block]
    for start in range(0, length, block):
        rows = slice(start, start + block)
        keys = kept_ref[rows, LANES : 2 * LANES]
        values = kept_ref[rows, 2 * LANES :]
        ktag = ktag_ref[rows, :]
        keys_of = (jnp.where(low_block, keys, ktag), jnp.where(low_block, ktag, keys))
        keys_f = keys.astype(F32)
        key_grad = value_grad = query_part = None
        for head in range(2):
            scores = mm(keys_of[head], queries_of[head], NT)
            probs = jnp.exp(scores - lse_ref[head : head + 1, :])
            prob_grad = mm(values, grads_of[head], NT)
            score_grad = (probs * (prob_grad - delta_of[head])).astype(BF)
            value_term = mm(probs.astype(BF), grads_of[head])
            key_term = mm(score_grad, clean_of[head])
            mine = low_block if head == 0 else jnp.logical_not(low_block)
            turned = jnp.transpose(jnp.where(mine, keys_f, 0.0)).astype(BF)
            query_term = mm(turned, score_grad)
            value_grad = value_term if head == 0 else value_grad + value_term
            key_grad = key_term if head == 0 else key_grad + key_term
            query_part = query_term if head == 0 else query_part + query_term
        acc_ref[...] = query_part if start == 0 else acc_ref[...] + query_part
        plain, crossed = turn(key_grad, cos_ref[rows, :], sin_ref[rows, :], front[:block])
        out_ref[rows, LANES : 2 * LANES] = (plain - crossed).astype(BF)
        out_ref[rows, 2 * LANES :] = value_grad.astype(BF)
    query_grad = jnp.transpose(acc_ref[...]) * (1.0 / math.sqrt(HEAD_DIM))
    plain, crossed = turn(query_grad, cos_ref[...], sin_ref[...], front)
    out_ref[:, :LANES] = (plain - crossed).astype(BF)


def several(body, count, shared, inputs, outputs, *refs):
    common = refs[count * inputs : count * inputs + shared]
    results = refs[count * inputs + shared : count * (inputs + outputs) + shared]
    scratch = refs[count * (inputs + outputs) + shared :]
    for at in range(count):
        body(
            *refs[at * inputs : (at + 1) * inputs],
            *common,
            *results[at * outputs : (at + 1) * outputs],
            *scratch,
        )


def call_pairs(body, pairs, common, out_shapes, scratch):
    count, inputs, outputs = len(pairs), len(pairs[0]), len(out_shapes)
    vmem = pl.BlockSpec(memory_space=pltpu.VMEM)
    flat = [array for pair in pairs for array in pair]
    results = pl.pallas_call(
        functools.partial(several, body, count, len(common), inputs, outputs),
        in_specs=[vmem] * (len(flat) + len(common)),
        out_specs=[vmem] * (outputs * count),
        out_shape=list(out_shapes) * count,
        scratch_shapes=scratch,
        compiler_params=pltpu.CompilerParams(vmem_limit_bytes=48 * 1024 * 1024),
        cost_estimate=pl.CostEstimate(flops=1024, bytes_accessed=1024, transcendentals=0),
    )(*flat, *common)
    return [tuple(results[at * outputs : (at + 1) * outputs]) for at in range(count)]


def prepare_kernel(
    ids, qkv_ref, gain_one, out_ref, inner_ref, gain_two, outer_ref,
    mine_ref, other_ref, rest_ref,
):
    on_zero = ids[0] == 0
    width = out_ref.shape[1]
    qkv = qkv_ref[...].astype(F32) * gain_one[...]
    for pair in range(width // 2 // LANES):
        for part in range(3):
            start = part * width + pair * LANES
            low = qkv[:, start : start + LANES]
            high = qkv[:, start + width // 2 : start + width // 2 + LANES]
            at = slice((pair * 3 + part) * LANES, (pair * 3 + part + 1) * LANES)
            mine_ref[:, at] = jnp.where(on_zero, low, high).astype(BF)
            other_ref[:, at] = jnp.where(on_zero, high, low).astype(BF)
    inner = (inner_ref[...].astype(F32) * gain_two[...]).astype(BF)
    gate, up, outer = inner[:, :FF], inner[:, FF:], outer_ref[...]
    blank = jnp.zeros((inner.shape[0], 2 * width - FF), BF)
    columns = (
        (out_ref[...], outer[:, :width]),
        (gate[:, :width], gate[:, width:], outer[:, width:]),
        (up[:, :width], up[:, width:], blank),
    )
    for route, parts in enumerate(columns):
        at = 0
        for part in parts:
            half, start = divmod(at, width)
            start += route * width
            rest_ref[half, :, start : start + part.shape[1]] = part
            at += part.shape[1]


def prepare(ids, qkv, gain_one, out_weight, inner, gain_two, outer):
    rows, width = out_weight.shape
    vmem = pl.BlockSpec(memory_space=pltpu.VMEM)
    return pl.pallas_call(
        prepare_kernel,
        in_specs=[pl.BlockSpec(memory_space=pltpu.SMEM)] + [vmem] * 6,
        out_specs=[vmem] * 3,
        out_shape=[
            jax.ShapeDtypeStruct((rows, 3 * width // 2), BF),
            jax.ShapeDtypeStruct((rows, 3 * width // 2), BF),
            jax.ShapeDtypeStruct((2, rows, 3 * width), BF),
        ],
        compiler_params=pltpu.CompilerParams(vmem_limit_bytes=32 * 1024 * 1024),
        cost_estimate=pl.CostEstimate(flops=1024, bytes_accessed=1024, transcendentals=0),
    )(ids, qkv, gain_one, out_weight, inner, gain_two, outer)


def attend(rows_of_pairs, tables):
    length = rows_of_pairs[0].shape[0]
    return call_pairs(
        functools.partial(attend_kernel, 512),
        [(rows,) for rows in rows_of_pairs],
        tables,
        [
            jax.ShapeDtypeStruct((length, 3 * LANES), BF),
            jax.ShapeDtypeStruct((length, LANES), BF),
            jax.ShapeDtypeStruct((2, length), F32),
        ],
        [],
    )


def attend_back_pairs(block, count, *refs):
    grad_ref, *tables = refs[3 * count : 3 * count + 5]
    out_ref, acc_ref = refs[3 * count + 5 :]
    for pair in range(count):
        kept_ref, ctx_ref, lse_ref = refs[3 * pair : 3 * pair + 3]
        attend_back_kernel(
            block,
            kept_ref,
            ctx_ref,
            grad_ref.at[:, pair * LANES : (pair + 1) * LANES],
            lse_ref,
            *tables,
            out_ref.at[:, 3 * pair * LANES : 3 * (pair + 1) * LANES],
            acc_ref,
        )


def attend_back(attended, heads_grad, tables):
    count, length = len(attended), heads_grad.shape[0]
    vmem = pl.BlockSpec(memory_space=pltpu.VMEM)
    return pl.pallas_call(
        functools.partial(attend_back_pairs, 512, count),
        in_specs=[vmem] * (3 * count + 5),
        out_specs=vmem,
        out_shape=jax.ShapeDtypeStruct((length, 3 * count * LANES), BF),
        scratch_shapes=[pltpu.VMEM((LANES, length), F32)],
        compiler_params=pltpu.CompilerParams(vmem_limit_bytes=48 * 1024 * 1024),
        cost_estimate=pl.CostEstimate(flops=1024, bytes_accessed=1024, transcendentals=0),
    )(*[array for pair in attended for array in pair], heads_grad, *tables)


def finish_kernel(ids, sums_ref, weight_ref, gain_ref, grad_ref, gain_grad_ref):
    on_zero = ids[0] == 0
    half = sums_ref.shape[1] // 2
    total = jnp.zeros((sums_ref.shape[0], LANES), F32)
    for pair in range(half // (3 * LANES)):
        for part in range(3):
            at = (pair * 3 + part) * LANES
            near, far = sums_ref[:, at : at + LANES], sums_ref[:, half + at : half + at + LANES]
            start = part * (half * 2 // 3) + pair * LANES
            for place, value in (
                (start, jnp.where(on_zero, near, far)),
                (start + half // 3, jnp.where(on_zero, far, near)),
            ):
                grad_ref[:, place : place + LANES] = value * gain_ref[...]
                total = total + value * weight_ref[:, place : place + LANES].astype(F32)
    gain_grad_ref[...] = jnp.sum(total, axis=1, keepdims=True)


def finish(ids, sums, weight, gain):
    vmem = pl.BlockSpec(memory_space=pltpu.VMEM)
    return pl.pallas_call(
        finish_kernel,
        in_specs=[pl.BlockSpec(memory_space=pltpu.SMEM)] + [vmem] * 3,
        out_specs=[vmem] * 2,
        out_shape=[
            jax.ShapeDtypeStruct(sums.shape, F32),
            jax.ShapeDtypeStruct((sums.shape[0], 1), F32),
        ],
        compiler_params=pltpu.CompilerParams(vmem_limit_bytes=32 * 1024 * 1024),
        cost_estimate=pl.CostEstimate(flops=1024, bytes_accessed=1024, transcendentals=0),
    )(ids, sums, weight, gain)


class Plan:
    def __init__(self, dp, ctx, seqs):
        self.dp, self.ctx = dp, ctx
        self.group = ctx // seqs
        self.fast = (dp, ctx, self.group) == (8, 4, 2)
        self.ctx_id = lax.axis_index("ctx")
        self.dp_id = lax.axis_index("dp")
        self.member = self.ctx_id % self.group
        self.seq = self.ctx_id // self.group

    def permute(self, array, target):
        pairs = []
        for dp in range(self.dp):
            for ctx in range(self.ctx):
                far_dp, far_ctx = target(dp, ctx)
                pairs.append((dp * self.ctx + ctx, far_dp * self.ctx + far_ctx))
        return lax.ppermute(array, AXES, pairs)

    def swap(self, array):
        return self.permute(array, lambda dp, ctx: (dp, (ctx + self.group) % self.ctx))

    def shift(self, array, step):
        size = self.group
        return self.permute(
            array, lambda dp, ctx: (dp, ctx // size * size + (ctx % size + step) % size)
        )

    def bit(self, name):
        if name in ("y", "core"):
            return self.ctx_id // 2 if name == "y" else self.ctx_id % 2
        return self.dp_id // {"zh": 4, "zl": 2, "x": 1}[name] % 2

    def cross(self, array, name):
        flip_dp = {"zh": 4, "zl": 2, "x": 1}.get(name, 0)
        flip_ctx = {"y": 2, "core": 1}.get(name, 0)
        return self.permute(array, lambda dp, ctx: (dp ^ flip_dp, ctx ^ flip_ctx))


ORDER = ("zh", "zl", "x", "y", "core")
ROUTES = (("zl", "x", "y"), ("x", "y", "zl"), ("y", "zl", "x"))
MLP_ROUTES = (("y", "zl", "x"), ("zl", "x", "y"), ("x", "y", "zl"))
QKV_ROUTES = (("y", "zl", "x"), ("zl", "x", "y"))


def in_order(mine, other, bit, axis):
    return jnp.where(
        bit == 0, jnp.stack([mine, other], axis=axis), jnp.stack([other, mine], axis=axis)
    )


def pick(array, index, axis):
    return lax.dynamic_index_in_dim(array, index, axis, keepdims=False)


def tie(*arrays):
    return lax.optimization_barrier(arrays)


class Pieces:
    def __init__(self, plan, array, bits):
        self.plan, self.array, self.bits = plan, array, bits

    def grow(self, name, *cuts):
        bits = [b for b in ORDER if b in self.bits or b == name]
        axis, bit = bits.index(name) + 1, self.plan.bit(name)
        theirs = self.plan.cross(self.array, name)
        ends = (0, *cuts, theirs.shape[-1])
        grown = [
            Pieces(
                self.plan,
                in_order(self.array[..., start:end], theirs[..., start:end], bit, axis),
                bits,
            )
            for start, end in zip(ends, ends[1:])
        ]
        return grown if cuts else grown[0]

    def shrink(self, name, last=False):
        axis, bit = self.bits.index(name), self.plan.bit(name)
        theirs = self.plan.cross(pick(self.array, 1 - bit, axis), name)
        total = pick(self.array, bit, axis).astype(F32) + theirs.astype(F32)
        return Pieces(
            self.plan, total if last else total.astype(BF), [b for b in self.bits if b != name]
        )

    def rows(self):
        return self.array.reshape(-1, self.array.shape[-1])


def tie_pieces(arrays, routes):
    tied = tie(*arrays, *[route.array for route in routes])
    count = len(arrays)
    return tied[:count], [Pieces(r.plan, h, r.bits) for r, h in zip(routes, tied[count:])]


def by_owner(plan, grad):
    return Pieces(plan, grad.reshape(2, 2, 2, 2, 2, -1, grad.shape[-1]), list(ORDER))


def group_columns(weight, group):
    rows = weight.shape[0]
    span = HEADS // group * HEAD_DIM
    padded = -(-span // LANES) * LANES
    split = weight.reshape(rows, 3, group, span)
    split = jnp.pad(split, ((0, 0), (0, 0), (0, 0), (0, padded - span)))
    split = split.reshape(rows, 3, group, padded // LANES, LANES)
    return jnp.transpose(split, (0, 2, 3, 1, 4)).reshape(rows, group, -1)


def ungroup_columns(weight):
    rows, group, width = weight.shape
    span = HEADS // group * HEAD_DIM
    pairs = width // (3 * LANES)
    split = jnp.transpose(weight.reshape(rows, group, pairs, 3, LANES), (0, 3, 1, 2, 4))
    split = split.reshape(rows, 3, group, pairs * LANES)[..., :span]
    return split.reshape(rows, 3 * HEADS * HEAD_DIM)


def own_rows(plan, grad, core):
    return pick(grad.reshape(2, 2, 2, 2, 2, -1, grad.shape[-1]), core, 4)


def scatter_all(grad):
    return lax.psum_scatter(grad.astype(F32), AXES, scatter_dimension=0, tiled=True)


def scatter_columns_all(plan, grad):
    spread = jnp.zeros((plan.group,) + grad.shape, F32)
    spread = lax.dynamic_update_index_in_dim(spread, grad.astype(F32), plan.member, 0)
    return scatter_all(ungroup_columns(jnp.transpose(spread, (1, 0, 2))))


def normalize(rows_in):
    row_mean = jnp.mean(rows_in, axis=-1, keepdims=True)
    centered = rows_in - row_mean
    variance = jnp.mean(centered * centered, axis=-1, keepdims=True)
    inv_std = lax.rsqrt(variance + EPS)
    return (centered * inv_std, inv_std)


def norm_back(scaled, normed, inv_std):
    return inv_std * (
        scaled
        - jnp.mean(scaled, axis=-1, keepdims=True)
        - normed * jnp.mean(scaled * normed, axis=-1, keepdims=True)
    )


def rope_tables(positions):
    lane = jnp.arange(LANES, dtype=jnp.int32)
    exponent = (lane % (HEAD_DIM // 2)).astype(F32) * (2.0 / HEAD_DIM)
    frequency = jnp.power(F32(THETA), -exponent)
    angles = positions.astype(F32)[:, None] * frequency
    sign = jnp.where(lane % HEAD_DIM < HEAD_DIM // 2, -1.0, 1.0)
    return jnp.cos(angles), jnp.sin(angles) * sign


def doc_tags(starts):
    lane = jnp.arange(LANES, dtype=jnp.int32) % HEAD_DIM
    used = lane < 2 * BITS
    bit = (starts[:, None] >> jnp.where(used, lane // 2, 0)) & 1
    odd = lane % 2
    query_on = used & (bit != odd)
    key_on = used & (bit == odd)
    return (
        jnp.where(query_on, FAR, 0.0).astype(BF),
        jnp.where(key_on, 1.0, 0.0).astype(BF),
    )


def shards(
    hidden_in,
    doc_positions,
    attn_gain,
    qkv_weight,
    out_weight,
    mlp_gain,
    inner_weight,
    outer_weight,
    grad_out,
    *,
    sizes,
):
    seqs, local, width = hidden_in.shape
    plan = Plan(*sizes, seqs)
    group, member = plan.group, plan.member
    other_seq = 1 - plan.seq

    def in_group(array):
        return [array] + [plan.shift(array, step) for step in range(1, group)]

    def pack(positions):
        rows = [
            jnp.concatenate([p // 256, p % 256, jnp.zeros(width - 2 * local, jnp.int32)])
            for p in positions
        ]
        return jnp.pad(jnp.stack(rows), ((0, 16 - len(rows)), (0, 0))).astype(BF)

    def unpack(rows):
        whole = rows.astype(jnp.int32)
        return whole[:local] * 256 + whole[local : 2 * local]

    own_hidden, far_hidden = pick(hidden_in, plan.seq, 0), pick(hidden_in, other_seq, 0)
    own_grad, far_grad = pick(grad_out, plan.seq, 0), pick(grad_out, other_seq, 0)
    own_marks, far_marks = pick(doc_positions, plan.seq, 0), pick(doc_positions, other_seq, 0)
    far_rows = jnp.concatenate(
        [far_hidden.astype(BF), far_grad.astype(BF), pack([far_marks])], axis=0
    )
    gain_one, gain_two = attn_gain.astype(F32)[:, None], mlp_gain.astype(F32)[:, None]
    outer_shard = jnp.transpose(outer_weight)
    pairs = -(-HEADS // group // 2)
    if plan.fast:
        core = plan.bit("core")
        mine, there, rest = prepare(
            core[None],
            qkv_weight,
            gain_one,
            out_weight,
            inner_weight,
            gain_two,
            outer_shard,
        )
        there, rest, far_rows = tie(there, rest, far_rows)
        there = plan.cross(there, "core")
        held = Pieces(plan, in_order(mine, there, core, 0), []).grow("zh")
        rest = Pieces(plan, rest, []).grow("zh")
        slim = 3 * LANES
        routes = []
        for at in range(3):
            parts = [held.array[..., at * slim : (at + 1) * slim]]
            parts += [rest.array[..., at * width : (at + 1) * width]]
            routes.append(Pieces(plan, jnp.concatenate(parts, axis=-1), held.bits))
        routes = [r.grow(ROUTES[at][0]) for at, r in enumerate(routes)]
        routes = [half for at, r in enumerate(routes) for half in r.grow(ROUTES[at][1], slim)]
    else:
        qkv_scaled = (qkv_weight.astype(F32) * gain_one).astype(BF)
        inner_scaled = (inner_weight.astype(F32) * gain_two).astype(BF)
        split = group_columns(qkv_scaled, group)
        whole = pick(lax.all_gather(split, AXES, axis=0, tiled=True), member, 1)
        qkv_columns = jnp.split(whole, pairs, axis=1)

    swapped = plan.swap(far_rows)
    rows_in = jnp.concatenate([own_hidden, swapped[:local].astype(F32)], axis=0)
    grad_rows = jnp.concatenate([own_grad, swapped[local : 2 * local].astype(F32)], axis=0)
    tokens = rows_in.shape[0]
    marks_own = [own_marks, unpack(swapped[2 * local])]
    normed_one, inv_one = normalize(rows_in)
    share = jnp.concatenate([normed_one.astype(BF), pack(marks_own)], axis=0)
    shared = in_group(share)
    if plan.fast:
        shared, routes = tie_pieces(shared, routes)
    first_in = jnp.concatenate([piece[:tokens] for piece in shared], axis=0)
    positions, starts = [], []
    for step, piece in enumerate(shared):
        marks = marks_own if step == 0 else [unpack(piece[tokens]), unpack(piece[tokens + 1])]
        block = plan.seq * group + (member - step) % group
        for at, mark in enumerate(marks):
            index = (block + at * group) % plan.ctx * local + jnp.arange(local, dtype=jnp.int32)
            positions.append(mark)
            starts.append(index - mark)
    cos_table, sine_table = rope_tables(jnp.concatenate(positions))
    qtag, ktag = doc_tags(jnp.concatenate(starts))
    tables = [cos_table, sine_table, qtag, ktag]

    if plan.fast:
        qkv_columns = [
            jnp.moveaxis(r.grow(ROUTES[at][2]).array, 0, 4).reshape(-1, slim)
            for at, r in enumerate(routes[::2])
        ]
        rest = routes[1::2]
        held, rest = tie_pieces([first_in, *tables, *qkv_columns], rest)
        first_in, tables, qkv_columns = held[0], list(held[1:5]), list(held[5:])
        theirs = [plan.cross(r.array, ROUTES[at][2]) for at, r in enumerate(rest)]
    qkv_rows = [mm(first_in, columns) for columns in qkv_columns]
    attended = []
    for rows in qkv_rows[:-1]:
        attended += attend([rows], tables)
    if plan.fast:
        held = tie(qkv_rows[2], *attended[0], *attended[1], *theirs)
        attended, theirs = [held[1:4], held[4:7]], held[7:]
        attended += attend([held[0]], tables)
        whole = []
        for at, r in enumerate(rest):
            name = ROUTES[at][2]
            axis, bit = ("zl", "x", "y").index(name) + 1, plan.bit(name)
            near, far = plan.cross(r.array, "core"), plan.cross(theirs[at], "core")
            both = [
                in_order(a, b, bit, axis + 1) for a, b in ((r.array, theirs[at]), (near, far))
            ]
            both = in_order(*both, core, 5).reshape(2, -1, width)
            whole += [both[0], both[1]]
    else:
        attended += attend(qkv_rows[-1:], tables)

    span = HEADS // group * HEAD_DIM

    def join_heads(pieces):
        if group == 2:
            return jnp.where(
                member == 0,
                jnp.concatenate(pieces, axis=1),
                jnp.concatenate(pieces[::-1], axis=1),
            )
        ring = jnp.concatenate(pieces + pieces, axis=1)
        return lax.dynamic_slice_in_dim(ring, (group - member) % group * span, group * span, 1)

    def heads_of(array, index):
        pieces = [array[:, at * span : (at + 1) * span] for at in range(group)]
        chosen = pieces[0]
        for at in range(1, group):
            chosen = jnp.where(index == at, pieces[at], chosen)
        return chosen

    def context_rows(step):
        rows = slice(step * tokens, (step + 1) * tokens)
        return jnp.concatenate([context[rows] for _, context, _ in attended], axis=1)[:, :span]

    context_b = join_heads(
        [context_rows(0)] + [plan.shift(context_rows(step), -step) for step in range(1, group)]
    )
    if plan.fast:
        thin = FF - width
        out_full = whole[0]
        outer_rows = jnp.concatenate([whole[1], whole[3][:, thin:]], axis=1)
        inner_gate = jnp.concatenate([whole[2], whole[3][:, :thin]], axis=1)
        inner_up = jnp.concatenate([whole[4], whole[5][:, :thin]], axis=1)
    else:
        out_full, outer_rows, inner_full = (
            lax.all_gather(w, AXES, axis=0, tiled=True)
            for w in (out_weight, outer_shard, inner_scaled)
        )
        inner_gate, inner_up = inner_full[:, :FF], inner_full[:, FF:]
    attn_part = mm(context_b, out_full)
    middle = rows_in + attn_part
    normed_two, inv_two = normalize(middle)
    second_in = normed_two.astype(BF)
    gate, up = mm(second_in, inner_gate), mm(second_in, inner_up)
    below = 0.5 * (1.0 + lax.erf(gate * math.sqrt(0.5)))
    bell = jnp.exp(-0.5 * gate * gate) * (1.0 / math.sqrt(2.0 * math.pi))
    gelu = gate * below
    gated = (gelu * up).astype(BF)
    branch_b = grad_rows.astype(BF)
    outer_grad = mm(branch_b, gated, TN).astype(BF)
    added = attn_part + mm(gated, outer_rows, NT)
    output_own = own_hidden + added[:local]
    added_far = added[local:].astype(BF)

    gated_grad = mm(branch_b, outer_rows)
    gate_grad = (gated_grad * up * (below + gate * bell)).astype(BF)
    up_grad = (gated_grad * gelu).astype(BF)
    inner_grad = [mm(second_in, gate_grad, TN).astype(BF), mm(second_in, up_grad, TN).astype(BF)]
    if plan.fast:
        mlp_routes = [by_owner(plan, g).shrink("core") for g in [outer_grad] + inner_grad]
    second_grad = mm(gate_grad, inner_gate, NT) + mm(up_grad, inner_up, NT)
    middle_part = norm_back(second_grad, normed_two, inv_two)
    attn_b = (grad_rows + middle_part).astype(BF)
    context_grad = mm(attn_b, out_full, NT).astype(BF)
    grad_pieces = [heads_of(context_grad, member)] + [
        plan.shift(heads_of(context_grad, (member + step) % group), step)
        for step in range(1, group)
    ]
    heads_grad = jnp.concatenate(grad_pieces, axis=0)
    heads_grad = jnp.pad(heads_grad, ((0, 0), (0, pairs * LANES - span)))
    out_grad = mm(context_b, attn_b, TN).astype(BF)

    def stage(routes, at, orders):
        return [r.shrink(orders[index][at]) for index, r in enumerate(routes)]

    if plan.fast:
        out_grad = by_owner(plan, out_grad).shrink("core").array
        sides = jnp.concatenate([mlp_routes[0].array, out_grad], axis=-1)
        mlp_routes[0] = Pieces(plan, sides, mlp_routes[0].bits)
        (heads_grad, added_far), mlp_routes = tie_pieces([heads_grad, added_far], mlp_routes)
        mlp_routes = stage(mlp_routes, 2, MLP_ROUTES)
    added_far = plan.swap(added_far)
    qkv_grad = attend_back(attended, heads_grad, tables)
    if plan.fast:
        (qkv_grad, added_far), mlp_routes = tie_pieces([qkv_grad, added_far], mlp_routes)
        weight_grad = mm(first_in, qkv_grad, TN).astype(BF)
        near = own_rows(plan, weight_grad, core)
        far = plan.cross(own_rows(plan, weight_grad, 1 - core), "core")
        attn_routes = [Pieces(plan, rows, list(ORDER[:4])) for rows in (near, far)]
        (qkv_grad,), routes = tie_pieces([qkv_grad], mlp_routes + attn_routes)
        attn_routes = stage(routes[3:], 2, QKV_ROUTES)
        mlp_routes = stage(routes[:3], 1, MLP_ROUTES)
    if plan.fast:
        (qkv_grad,), routes = tie_pieces([qkv_grad], mlp_routes + attn_routes)
        attn_routes = stage(routes[3:], 1, QKV_ROUTES)
        mlp_routes = stage(routes[:3], 0, MLP_ROUTES)
    output_far = far_hidden + added_far.astype(F32)
    first_part = mm(qkv_grad, jnp.concatenate(qkv_columns, axis=1), NT)
    first_grad = first_part[:tokens]
    for step in range(1, group):
        piece = first_part[step * tokens : (step + 1) * tokens].astype(BF)
        first_grad = first_grad + plan.shift(piece, -step).astype(F32)
    if plan.fast:
        (first_grad,), routes = tie_pieces([first_grad], mlp_routes + attn_routes)
        mlp_routes, attn_routes = routes[:3], routes[3:]
    grad_added = middle_part + norm_back(first_grad, normed_one, inv_one)
    input_own = own_grad + grad_added[:local]
    input_far = far_grad + plan.swap(grad_added[local:].astype(BF)).astype(F32)

    if plan.fast:
        attn_routes = stage(attn_routes, 0, QKV_ROUTES)
        mlp_sum = Pieces(
            plan, jnp.concatenate([r.array for r in mlp_routes], axis=-1), ["zh"]
        ).shrink("zh", last=True).array
        attn_sum = Pieces(
            plan, jnp.concatenate([r.array for r in attn_routes], axis=-1), ["zh"]
        ).shrink("zh", last=True).array
        outer_sum, out_sum = mlp_sum[:, :FF], mlp_sum[:, FF : FF + width]
        inner_sum = mlp_sum[:, FF + width :]
        qkv_out, gain_out = finish(core[None], attn_sum, qkv_weight, gain_one)
        gain_out = gain_out.reshape(-1)
    else:
        out_sum, outer_sum = scatter_all(out_grad), scatter_all(outer_grad)
        inner_sum = scatter_all(jnp.concatenate(inner_grad, axis=1))
        qkv_sum = scatter_columns_all(plan, mm(first_in, qkv_grad, TN))
        qkv_out = qkv_sum * gain_one
        gain_out = jnp.sum(qkv_sum * qkv_weight.astype(F32), axis=1)
    return (
        in_order(output_own, output_far, plan.seq, 0),
        in_order(input_own, input_far, plan.seq, 0),
        gain_out,
        qkv_out,
        out_sum,
        jnp.sum(inner_sum * inner_weight.astype(F32), axis=1),
        inner_sum * gain_two,
        jnp.transpose(outer_sum),
    )


def solution(mesh):
    sizes = (mesh.shape["dp"], mesh.shape["ctx"])
    return jax.shard_map(
        functools.partial(shards, sizes=sizes),
        mesh=mesh,
        in_specs=(
            P("dp", "ctx", None),
            P("dp", "ctx"),
            P(AXES),
            P(AXES, None),
            P(AXES, None),
            P(AXES),
            P(AXES, None),
            P(None, AXES),
            P("dp", "ctx", None),
        ),
        out_specs=(
            P("dp", "ctx", None),
            P("dp", "ctx", None),
            P(AXES),
            P(AXES, None),
            P(AXES, None),
            P(AXES),
            P(AXES, None),
            P(None, AXES),
        ),
        check_vma=False,
    )
```
